256 devices in a mesh: grp: 16 (over y, z_lo), tp: 16 (over z_hi, x, core).
Axes of the slice: x: 4, y: 4, z: 8 (z_hi: 2, z_lo: 4; z = z_hi * 4 + z_lo), core: 2. Of those that a mesh axis runs over, the one named last changes fastest.
Arguments:
- pre_act: bfloat16 [16, 2048, 4096], P('grp', None, 'tp'), may hold values from -6 to 6
- cotangent: bfloat16 [16, 2048, 2048], P('grp', 'tp'), may hold values from -6 to 6
- w_down: bfloat16 [16, 4096, 2048], P('grp', 'tp'), may hold values from -0.09375 to 0.09375
- first_moment: float32 [16, 4096, 2048], P('grp', 'tp'), may hold values from -4 to 4
- second_moment: float32 [16, 4096, 2048], P('grp', 'tp'), may hold values from 0.05 to 2
- path_table: int32 [16], replicated, may hold values from 0 to 15, as said below
- sharer_counts: int32 [16], replicated, may hold values from 0 to 8, as said below
Outputs:
- grad_avg: bfloat16 [16, 4096, 2048], P('grp', 'tp')
- first_avg: float32 [16, 4096, 2048], P('grp', 'tp')
- second_avg: float32 [16, 4096, 2048], P('grp', 'tp')
- pre_grad: bfloat16 [16, 2048, 4096], P('grp', None, 'tp')
The draws below stay inside these ranges and needn't reach their ends.
Inputs may be any that keep to these rules, and one draw needn't show every extreme that they name: `path_table`: exactly 8 groups have module 16 - 1 and exactly one group has module 0. `sharer_counts`: entry m is the number of entries of path_table equal to m.
All inputs are finite; a program needn't handle non-finite values.
Results may differ from the reference program's by a relative error of at most 0.0051.
Values may be sent and summed in bfloat16 or wider, within the bound.
A program may use at most 128 MiB of HBM per device.

```python
import math
import jax
import jax.numpy as jnp
from jax import lax

D = 2048
FF = 4096
MODULES = 16
TOK_GRP = 2048
GROUPS = 16


def shared_paths(key):
    pick_key, shuffle_key = jax.random.split(key)
    others = jax.random.randint(pick_key, (GROUPS,), 1, MODULES - 1, dtype=jnp.int32)
    shuffle = jax.random.permutation(shuffle_key, GROUPS)
    ranks = jnp.arange(GROUPS, dtype=jnp.int32)
    half = GROUPS // 2
    by_rank = jnp.where(ranks < half, MODULES - 1, jnp.where(ranks == half, 0, others)).astype(jnp.int32)
    path_ids = jnp.zeros((GROUPS,), jnp.int32).at[shuffle].set(by_rank)
    return path_ids.astype(jnp.int32)


def draw_path_table(key, part):
    return shared_paths(key)


def draw_sharer_counts(key, part):
    path_ids = shared_paths(key)
    module_ids = jnp.arange(MODULES, dtype=jnp.int32)
    matches = (path_ids[:, None] == module_ids[None, :]).astype(jnp.int32)
    return jnp.sum(matches, axis=0).astype(jnp.int32)


def shard_levels(own_key, dims, pieces, low, largest):
    factor_of, own = 1.0, jax.random.fold_in(own_key, 6)
    for dim, blocks in pieces:
        heights = jnp.exp(jax.random.uniform(jax.random.fold_in(own, dim), (blocks,), jnp.float32, low / len(pieces), largest / len(pieces)))
        factor_of = factor_of * jnp.repeat(heights, dims[dim] // blocks).reshape([-1 if axis == dim else 1 for axis in range(len(dims))])
    return factor_of


def noise(stream_key, dims, width, most, cuts=(), held_as=jnp.bfloat16):
    values = jax.random.normal(stream_key, dims, jnp.float32) * width
    if len(cuts) > 0:
        values = shard_levels(stream_key, dims, cuts, -0.22, 0.18) * values
    return jnp.clip(values, min=-most, max=most).astype(held_as)


def setup_inputs(seed: int = 0) -> dict:
    keys = jax.random.split(jax.random.key(seed), 8)
    pre_act = noise(keys[0], (GROUPS, TOK_GRP, FF), 1.0, 6.0, ((0, 16), (2, 16)))
    cotangent = noise(keys[1], (GROUPS, TOK_GRP, D), 1.0, 6.0, ((0, 16), (1, 16)))
    w_down = noise(keys[2], (GROUPS, FF, D), FF ** -0.5, 0.09375, ((0, 16), (1, 16)))
    first_moment = noise(keys[3], (GROUPS, FF, D), 0.5, 4.0, ((0, 16), (1, 16)), jnp.float32)
    second_moment = jnp.clip(jnp.exp(math.log(2.0) - 3.6888794 * jax.random.uniform(keys[4], (GROUPS, FF, D), jnp.float32) ** shard_levels(keys[4], (GROUPS, FF, D), ((0, 16), (1, 16)), -0.2, 0.2)), 0.05, 2.0)
    path_table = draw_path_table(jax.random.fold_in(keys[7], 71), 0)
    sharer_counts = draw_sharer_counts(jax.random.fold_in(keys[7], 71), 0)
    return {"pre_act": pre_act, "cotangent": cotangent, "w_down": w_down, "first_moment": first_moment, "second_moment": second_moment, "path_table": path_table, "sharer_counts": sharer_counts}


def reference(pre_act, cotangent, w_down, first_moment, second_moment, path_table, sharer_counts):
    inv_root_two = 1.0 / math.sqrt(2.0)
    inv_root_tau = 1.0 / math.sqrt(2.0 * math.pi)
    token_scale = 1.0 / math.sqrt(TOK_GRP)

    def one_group(operands):
        inputs_bf, grads_bf, weights = operands
        inputs = inputs_bf.astype(jnp.float32)
        normal_cdf = 0.5 * (1.0 + jax.scipy.special.erf(inputs * inv_root_two))
        hidden = (inputs * normal_cdf).astype(jnp.bfloat16)
        gradient_slope = normal_cdf + inputs * jnp.exp(-0.5 * inputs * inputs) * inv_root_tau
        gradient = jnp.dot(hidden.T, grads_bf, preferred_element_type=jnp.float32) * token_scale
        back_rows = jnp.dot(grads_bf, weights.T, preferred_element_type=jnp.float32)
        return (gradient, (back_rows * gradient_slope).astype(jnp.bfloat16))
    gradient, pre_grad = lax.map(one_group, (pre_act, cotangent, w_down))
    moment_one = 0.9 * first_moment + 0.1 * gradient
    moment_two = 0.95 * second_moment + 0.05 * gradient * gradient
    shared = (path_table[:, None] == path_table[None, :]).astype(jnp.float32)
    divisor = sharer_counts[path_table].astype(jnp.float32)

    def average(values):
        summed = jnp.einsum('gh,hfd->gfd', shared, values, precision=lax.Precision.HIGHEST)
        return summed / divisor[:, None, None]
    grad_avg = average(gradient).astype(jnp.bfloat16)
    return (grad_avg, average(moment_one), average(moment_two), pre_grad)
```

```python
import functools
import math

import jax
import jax.numpy as jnp
from jax import lax
from jax.experimental import pallas as pl
from jax.experimental.pallas import tpu as pltpu
from jax.sharding import PartitionSpec as P

MESH = pl.DeviceIdType.MESH
COLS = 256
NY = 4
NZ = 4
NX = 4
SLOTS = 4
LAG_END, LAG_MID, LAG_AVG, LAG_RET, LAG_OUT = 2, 4, 6, 8, 10

INV_ROOT_TWO = 1.0 / math.sqrt(2.0)
INV_ROOT_TAU = 1.0 / math.sqrt(2.0 * math.pi)


def kernel(
    chunks, block, quarter, scale,
    table, pre_act, cot, w_down, first, second,
    grad_out, first_out, second_out, pre_out,
    gbuf, hid_t, slope, grad, mine, raw, slots, from_end, from_mid, avg, back, ret,
    cot_send, group_send, z_sem, x_sem, c_sem, raw_sem, end_sem, mid_sem, ret_sem,
):
    f32, bf16 = jnp.float32, jnp.bfloat16
    units = 3 * chunks
    g, t = lax.axis_index("grp"), lax.axis_index("tp")
    y, zl = g // NZ, lax.rem(g, NZ)
    zh, x, core = t // (2 * NX), lax.rem(t // 2, NX), lax.rem(t, 2)
    is_mid = jnp.logical_or(zl == 1, zl == 2)
    mate = jnp.where(is_mid, jnp.where(zl == 1, 0, 3), jnp.where(zl == 0, 1, 2))
    mate_id = (y * NZ + mate, t)
    mid_id = (y * NZ + 3 - zl, t)
    y_ids = [(lax.rem(y + d, NY) * NZ + zl, t) for d in (1, 2, 3)]
    x_ids = [(g, zh * 2 * NX + lax.rem(x + d, NX) * 2 + core) for d in (1, 3, 2)]
    z_id = (g, (1 - zh) * 2 * NX + x * 2 + core)
    c_id = (g, zh * 2 * NX + x * 2 + 1 - core)

    pair_at = pl.multiple_of((core * NX + x) * 2 * block, 2 * block)
    own_at = pl.multiple_of(pair_at + zh * block, block)
    half_at = pl.multiple_of(core * NX * 2 * block, NX * 2 * block)

    barrier = pltpu.get_barrier_semaphore()
    for peer in [z_id, c_id, mate_id] + x_ids + y_ids:
        pl.semaphore_signal(barrier, inc=1, device_id=peer, device_id_type=MESH)

    @pl.when(is_mid)
    def _():
        pl.semaphore_signal(barrier, inc=1, device_id=mid_id, device_id_type=MESH)

    for c in range(chunks):
        gbuf[c, pl.ds(own_at, block), :] = cot[:, c * COLS:(c + 1) * COLS]

    pl.semaphore_wait(barrier, jnp.where(is_mid, 10, 9))

    def send(src, dst, ssem, rsem, peer):
        pltpu.make_async_remote_copy(
            src_ref=src, dst_ref=dst, send_sem=ssem, recv_sem=rsem,
            device_id=peer, device_id_type=MESH,
        ).start()

    def wait(ref, sem):
        pltpu.make_async_copy(ref, ref, sem).wait()

    def columns(c):
        return pl.ds(pl.multiple_of(c * COLS, COLS), COLS)

    def quarter_rows(owner):
        return pl.ds(pl.multiple_of(owner * quarter, quarter), quarter)

    def send_raw(u):
        for d in range(3):
            owner = lax.rem(y + d + 1, NY)
            send(mine.at[u, quarter_rows(owner)], raw.at[u, d], group_send.at[0], raw_sem.at[u], y_ids[d])

    def column_slots(u, r):
        parts = [mine[u, pl.ds(pl.multiple_of(y * quarter + r * 16, 16), 16), :].astype(f32)]
        parts += [raw[u, d, pl.ds(r * 16, 16), :].astype(f32) for d in range(3)]
        group = [lax.rem(y - d + NY, NY) * NZ + zl for d in range(4)]
        out = []
        for s in range(SLOTS):
            total = table[s * 16 + group[0]] * parts[0]
            for d in range(1, 4):
                total += table[s * 16 + group[d]] * parts[d]
            out.append(total)
        return out

    def send_back(u, held, scaled):
        for r in range(quarter // 16):
            rows = pl.ds(r * 16, 16)
            parts = [held[u, s, rows, :].astype(f32) for s in range(SLOTS)]
            for d in range(4):
                group = lax.rem(y + d, NY) * NZ + zl
                total = table[group] * parts[0]
                for s in range(1, SLOTS):
                    total += table[s * 16 + group] * parts[s]
                if d == 0:
                    ret[u, pl.ds(pl.multiple_of(y * quarter + r * 16, 16), 16), :] = total.astype(bf16)
                else:
                    back[u, d - 1, rows, :] = total.astype(bf16)
        for d in range(3):
            send(back.at[u, d], ret.at[u, quarter_rows(y)], group_send.at[2], ret_sem.at[u], y_ids[d])

    def tick(i, carry):
        @pl.when(jnp.logical_and(lax.rem(i, 2) == 0, i < 2 * chunks))
        def _():
            c = i // 2
            part = gbuf.at[c, pl.ds(own_at, block)]
            send(part, part, cot_send.at[0], z_sem.at[c], z_id)

        @pl.when(jnp.logical_and(lax.rem(i, 2) == 1, i < 2 * chunks + 1))
        def _():
            c = i // 2
            wait(gbuf.at[c, pl.ds(own_at, block)], z_sem.at[c])
            part = gbuf.at[c, pl.ds(pair_at, 2 * block)]
            for k in range(3):
                send(part, part, cot_send.at[1], x_sem.at[c], x_ids[k])

        @pl.when(jnp.logical_and(lax.rem(i, 2) == 0, jnp.logical_and(i >= 4, i < 2 * chunks + 4)))
        def _():
            c = i // 2 - 2
            wait(gbuf.at[c, pl.ds(0, 6 * block)], x_sem.at[c])
            part = gbuf.at[c, pl.ds(half_at, NX * 2 * block)]
            send(part, part, cot_send.at[2], c_sem.at[c], c_id)

        @pl.when(i < chunks)
        def _():
            mine[i] = first[:, columns(i)].astype(bf16)
            send_raw(i)
            place_core, place_x = i // NX, lax.rem(i, NX)
            for half in range(2):
                rows = pl.ds(pl.multiple_of((half * 2 * NX + place_x * 2 + place_core) * block, block), block)
                put = pl.ds(pl.multiple_of((i * 2 + half) * block, block), block)
                inputs = pre_act[rows, :].astype(f32)
                cdf = 0.5 * (1.0 + lax.erf(inputs * INV_ROOT_TWO))
                slope[put, :] = cdf + inputs * jnp.exp(-0.5 * inputs * inputs) * INV_ROOT_TAU
                hid_t[:, put] = (inputs * cdf).T.astype(bf16)

        @pl.when(jnp.logical_and(i >= chunks, jnp.logical_and(i < units, lax.rem(i - chunks, 2) == 0)))
        def _():
            c = (i - chunks) // 2
            wait(gbuf.at[c, pl.ds(0, NX * 2 * block)], c_sem.at[c])
            value = jnp.dot(hid_t[...], gbuf[c], preferred_element_type=f32) * scale
            grad[c] = value
            mine[i] = value.astype(bf16)
            send_raw(i)

        @pl.when(jnp.logical_and(i >= chunks, jnp.logical_and(i < units, lax.rem(i - chunks, 2) == 1)))
        def _():
            c = (i - chunks) // 2
            value = grad[c]
            mine[i] = (0.95 * second[:, columns(c)] + 0.05 * value * value).astype(bf16)
            send_raw(i)

        u = i - LAG_END

        @pl.when(jnp.logical_and(jnp.logical_not(is_mid), jnp.logical_and(u >= 0, u < units)))
        def _():
            wait(raw.at[u], raw_sem.at[u])
            for r in range(quarter // 16):
                sums = column_slots(u, r)
                for s in range(SLOTS):
                    slots[u, s, pl.ds(r * 16, 16), :] = sums[s].astype(bf16)
            send(slots.at[u], from_end.at[u], group_send.at[1], end_sem.at[u], mate_id)

        m = i - LAG_MID

        @pl.when(jnp.logical_and(is_mid, jnp.logical_and(m >= 0, m < units)))
        def _():
            wait(raw.at[m], raw_sem.at[m])
            wait(from_end.at[m], end_sem.at[m])
            for r in range(quarter // 16):
                sums = column_slots(m, r)
                for s in range(SLOTS):
                    rows = pl.ds(r * 16, 16)
                    slots[m, s, rows, :] = (sums[s] + from_end[m, s, rows, :].astype(f32)).astype(bf16)
            send(slots.at[m], from_mid.at[m], group_send.at[1], mid_sem.at[m], mid_id)

        v = i - LAG_AVG

        @pl.when(jnp.logical_and(is_mid, jnp.logical_and(v >= 0, v < units)))
        def _():
            wait(from_mid.at[v], mid_sem.at[v])
            for r in range(quarter // 16):
                rows = pl.ds(r * 16, 16)
                for s in range(SLOTS):
                    total = slots[v, s, rows, :].astype(f32) + from_mid[v, s, rows, :].astype(f32)
                    avg[v, s, rows, :] = (table[64 + s] * total).astype(bf16)
            send(avg.at[v], from_end.at[v], group_send.at[3], end_sem.at[v], mate_id)
            send_back(v, avg, True)

        b = i - LAG_RET

        @pl.when(jnp.logical_and(jnp.logical_not(is_mid), jnp.logical_and(b >= 0, b < units)))
        def _():
            wait(from_end.at[b], end_sem.at[b])
            send_back(b, from_end, False)

        o = i - LAG_OUT
        alone = table[80 + g]

        @pl.when(jnp.logical_and(o >= 0, o < units))
        def _():
            wait(raw.at[o], ret_sem.at[o])

        @pl.when(jnp.logical_and(o >= chunks, jnp.logical_and(o < units, lax.rem(o - chunks, 2) == 0)))
        def _():
            c = (o - chunks) // 2
            cols = columns(c)
            for r in range(4):
                rows = pl.ds(r * quarter, quarter)
                own = grad[c, rows, :]
                mean = ret[o, rows, :].astype(f32)
                grad_out[rows, cols] = (mean + alone * own).astype(bf16)
                first_out[rows, cols] = (
                    0.9 * ret[c, rows, :].astype(f32) + 0.1 * mean
                    + alone * (0.9 * first[rows, cols] + 0.1 * own)
                )

        @pl.when(jnp.logical_and(o >= chunks, jnp.logical_and(o < units, lax.rem(o - chunks, 2) == 1)))
        def _():
            c = (o - chunks) // 2
            cols = columns(c)
            for r in range(4):
                rows = pl.ds(r * quarter, quarter)
                own = grad[c, rows, :]
                second_out[rows, cols] = ret[o, rows, :].astype(f32) + alone * (
                    0.95 * second[rows, cols] + 0.05 * own * own
                )

        p = i - (units - 1)

        @pl.when(jnp.logical_and(p >= 0, p < 2 * NX))
        def _():
            here = pl.ds(pl.multiple_of(p * 2 * block, 2 * block), 2 * block)
            total = jnp.zeros((2 * block, pre_act.shape[1]), f32)
            for c in range(chunks):
                total += lax.dot_general(
                    gbuf[c, here, :], w_down[:, c * COLS:(c + 1) * COLS],
                    (((1,), (1,)), ((), ())), preferred_element_type=f32,
                )
            total = (total * slope[here, :]).astype(bf16)
            place_core, place_x = p // NX, lax.rem(p, NX)
            for half in range(2):
                rows = pl.ds(pl.multiple_of((half * 2 * NX + place_x * 2 + place_core) * block, block), block)
                pre_out[rows, :] = total[half * block:(half + 1) * block]

        return carry

    lax.fori_loop(0, units + LAG_OUT, tick, 0)

    wait(gbuf.at[:, pl.ds(0, block)], cot_send.at[0])
    wait(gbuf.at[:, pl.ds(0, 6 * block)], cot_send.at[1])
    wait(gbuf.at[:, pl.ds(0, 2 * NX * block)], cot_send.at[2])
    wait(raw, group_send.at[0])
    wait(slots, group_send.at[1])
    wait(raw, group_send.at[2])

    @pl.when(is_mid)
    def _():
        wait(avg, group_send.at[3])


def sharing_table(path_table, sharer_counts):
    f32 = jnp.float32
    ids = jnp.arange(path_table.shape[0], dtype=jnp.int32)
    same = path_table[:, None] == path_table[None, :]
    leader = jnp.min(jnp.where(same, ids[None, :], ids.shape[0]), axis=1)
    shared = jnp.sum(same.astype(jnp.int32), axis=1) > 1
    opens = jnp.logical_and(shared, leader == ids)
    slot = jnp.sum(jnp.logical_and(opens[None, :], ids[None, :] < leader[:, None]).astype(jnp.int32), axis=1)
    member = jnp.logical_and(shared[None, :], slot[None, :] == jnp.arange(SLOTS, dtype=jnp.int32)[:, None])
    modules = jnp.arange(sharer_counts.shape[0], dtype=jnp.int32)
    lookup = path_table[:, None] == modules[None, :]
    count = jnp.sum(jnp.where(lookup, sharer_counts[None, :], 0), axis=1).astype(f32)
    inverse = jnp.max(jnp.where(member, 1.0 / count[None, :], 0.0), axis=1)
    alone = jnp.where(shared, 0.0, 1.0 / count)
    rows = [member.astype(f32).reshape(-1), jnp.pad(inverse, (0, 16 - SLOTS)), alone]
    return jnp.concatenate(rows)


def per_device(pre_act, cotangent, w_down, first_moment, second_moment, path_table, sharer_counts):
    f32, bf16 = jnp.float32, jnp.bfloat16
    block, width = cotangent.shape[1:]
    tokens, hidden = pre_act.shape[1:]
    chunks, quarter = width // COLS, hidden // NY
    units = 3 * chunks
    table = sharing_table(path_table, sharer_counts)
    vmem = pl.BlockSpec(memory_space=pltpu.VMEM)
    held = pltpu.VMEM((units, SLOTS, quarter, COLS), bf16)
    ring = pltpu.VMEM((units, 3, quarter, COLS), bf16)
    whole = pltpu.VMEM((units, hidden, COLS), bf16)
    outs = pl.pallas_call(
        functools.partial(kernel, chunks, block, quarter, 1.0 / math.sqrt(tokens)),
        out_shape=(
            jax.ShapeDtypeStruct((hidden, width), bf16),
            jax.ShapeDtypeStruct((hidden, width), f32),
            jax.ShapeDtypeStruct((hidden, width), f32),
            jax.ShapeDtypeStruct((tokens, hidden), bf16),
        ),
        in_specs=[pl.BlockSpec(memory_space=pltpu.SMEM)] + [vmem] * 5,
        out_specs=(vmem,) * 4,
        scratch_shapes=[
            pltpu.VMEM((chunks, tokens, COLS), bf16),
            pltpu.VMEM((hidden, tokens), bf16),
            pltpu.VMEM((tokens, hidden), f32),
            pltpu.VMEM((chunks, hidden, COLS), f32),
            whole,
            ring,
            held,
            held,
            held,
            held,
            ring,
            whole,
            pltpu.SemaphoreType.DMA((3,)),
            pltpu.SemaphoreType.DMA((4,)),
            pltpu.SemaphoreType.DMA((chunks,)),
            pltpu.SemaphoreType.DMA((chunks,)),
            pltpu.SemaphoreType.DMA((chunks,)),
            pltpu.SemaphoreType.DMA((units,)),
            pltpu.SemaphoreType.DMA((units,)),
            pltpu.SemaphoreType.DMA((units,)),
            pltpu.SemaphoreType.DMA((units,)),
        ],
        compiler_params=pltpu.CompilerParams(
            collective_id=0, has_side_effects=True, vmem_limit_bytes=60 * 2**20
        ),
        cost_estimate=pl.CostEstimate(
            flops=4 * tokens * hidden * width, bytes_accessed=13 * 2**20, transcendentals=2 * tokens * hidden
        ),
        name="routed_down_grad",
    )(table, pre_act[0], cotangent[0], w_down[0], first_moment[0], second_moment[0])
    return tuple(out[None] for out in outs)


def solution(mesh):
    placed = (
        P("grp", None, "tp"),
        P("grp", "tp", None),
        P("grp", "tp", None),
        P("grp", "tp", None),
        P("grp", "tp", None),
        P(),
        P(),
    )
    return jax.shard_map(
        per_device,
        mesh=mesh,
        in_specs=placed,
        out_specs=(
            P("grp", "tp", None),
            P("grp", "tp", None),
            P("grp", "tp", None),
            P("grp", None, "tp"),
        ),
        check_vma=False,
    )
```

```python
import functools
import math

import jax
import jax.numpy as jnp
from jax import lax
from jax.experimental import pallas as pl
from jax.experimental.pallas import tpu as pltpu
from jax.sharding import PartitionSpec as P

MESH = pl.DeviceIdType.MESH
COLS = 256
NY = 4
NZ = 4
NX = 4
FEWEST_SLOTS, MOST_SLOTS = 2, 4
LAG_END, LAG_MID, LAG_AVG, LAG_RET = 3, 6, 9, 12

B_AT, C_AT = 2, 7
AHEAD = 2
STEPS = 4

INV_ROOT_TWO = 1.0 / math.sqrt(2.0)
INV_ROOT_TAU = 1.0 / math.sqrt(2.0 * math.pi)


def kernel(
    nslots, chunks, block, quarter, scale,
    path, counts, pre_act_in, cot_in, w_down_in, first_in, second_in,
    ret, pre_out,
    table, pre_act, cot, w_down, first, second,
    gbuf, hid_t, slope, grad, mine, raw, slots, from_end, from_mid, avg, back, pre,
    load_sem, store_sem, cot_send, group_send, z_sem, x_sem, c_sem, raw_sem, end_sem, mid_sem, ret_sem,
):
    f32, bf16 = jnp.float32, jnp.bfloat16
    units = 3 * chunks
    g, t = lax.axis_index("grp"), lax.axis_index("tp")
    y, zl = g // NZ, lax.rem(g, NZ)
    zh, x, core = t // (2 * NX), lax.rem(t // 2, NX), lax.rem(t, 2)
    is_mid = jnp.logical_or(zl == 1, zl == 2)
    mate = jnp.where(is_mid, jnp.where(zl == 1, 0, 3), jnp.where(zl == 0, 1, 2))
    mate_id = (y * NZ + mate, t)
    mid_id = (y * NZ + 3 - zl, t)
    y_ids = [(lax.rem(y + d, NY) * NZ + zl, t) for d in (1, 2, 3)]
    x_ids = [(g, zh * 2 * NX + lax.rem(x + d, NX) * 2 + core) for d in (1, 3, 2)]
    z_id = (g, (1 - zh) * 2 * NX + x * 2 + core)
    c_id = (g, zh * 2 * NX + x * 2 + 1 - core)

    pair_at = pl.multiple_of((core * NX + x) * 2 * block, 2 * block)
    own_at = pl.multiple_of(pair_at + zh * block, block)
    other_at = pl.multiple_of(pair_at + (1 - zh) * block, block)
    half_at = pl.multiple_of(core * NX * 2 * block, NX * 2 * block)

    barrier = pltpu.get_barrier_semaphore()
    for peer in [z_id, c_id, mate_id] + x_ids + y_ids:
        pl.semaphore_signal(barrier, inc=1, device_id=peer, device_id_type=MESH)

    @pl.when(is_mid)
    def _():
        pl.semaphore_signal(barrier, inc=1, device_id=mid_id, device_id_type=MESH)

    loads = [(cot_in, cot), (first_in, first), (pre_act_in, pre_act), (second_in, second), (w_down_in, w_down)]
    loads = [pltpu.make_async_copy(src, dst, load_sem.at[k]) for k, (src, dst) in enumerate(loads)]
    for load in loads:
        load.start()
    fill_table(nslots, table, path, counts)
    loads[0].wait()
    for c in range(chunks):
        gbuf[c, pl.ds(own_at, block), :] = cot[:, c * COLS:(c + 1) * COLS]

    pl.semaphore_wait(barrier, jnp.where(is_mid, 10, 9))

    def send(src, dst, ssem, rsem, peer):
        pltpu.make_async_remote_copy(
            src_ref=src, dst_ref=dst, send_sem=ssem, recv_sem=rsem,
            device_id=peer, device_id_type=MESH,
        ).start()

    def wait(ref, sem):
        pltpu.make_async_copy(ref, ref, sem).wait()

    def columns(c):
        return pl.ds(pl.multiple_of(c * COLS, COLS), COLS)

    def quarter_rows(owner):
        return pl.ds(pl.multiple_of(owner * quarter, quarter), quarter)

    def send_x(c, at):
        part = gbuf.at[c, pl.ds(at, block)]
        for k in range(3):
            send(part, part, cot_send.at[1], x_sem.at[c], x_ids[k])

    def send_own(c):
        part = gbuf.at[c, pl.ds(own_at, block)]
        send(part, part, cot_send.at[0], z_sem.at[c], z_id)
        send_x(c, own_at)

    def send_raw(u):
        for d in range(3):
            owner = lax.rem(y + d + 1, NY)
            send(mine.at[u, quarter_rows(owner)], raw.at[u, d], group_send.at[0], raw_sem.at[u], y_ids[d])

    def column_parts(u, r):
        parts = [mine[u, pl.ds(pl.multiple_of(y * quarter + r * 16, 16), 16), :].astype(f32)]
        return parts + [raw[u, d, pl.ds(r * 16, 16), :].astype(f32) for d in range(3)]

    def column_slots(u, r):
        parts = column_parts(u, r)
        group = [lax.rem(y - d + NY, NY) * NZ + zl for d in range(4)]
        out = []
        for s in range(nslots):
            total = table[s * 16 + group[0]] * parts[0]
            for d in range(1, 4):
                total += table[s * 16 + group[d]] * parts[d]
            out.append(total)
        return out

    def send_back(u, held):
        for r in range(quarter // 16):
            rows = pl.ds(r * 16, 16)
            own = column_parts(u, r)
            parts = [held[u, s, rows, :].astype(f32) for s in range(nslots)]
            for d in range(4):
                group = lax.rem(y + d, NY) * NZ + zl
                total = table[group] * parts[0]
                for s in range(1, nslots):
                    total += table[s * 16 + group] * parts[s]
                for k in range(4):
                    total += table[80 + group * NY + lax.rem(y - k + NY, NY)] * own[k]
                back[u, d, rows, :] = total.astype(bf16)
        pltpu.make_async_copy(back.at[u, 0], ret.at[u, quarter_rows(y)], store_sem.at[0]).start()
        for d in range(3):
            send(back.at[u, d + 1], ret.at[u, quarter_rows(y)], group_send.at[2], ret_sem.at[0], y_ids[d])

    def tick(i, carry):
        @pl.when(i < chunks)
        def _():
            mine[i] = first[:, columns(i)].astype(bf16)
            send_raw(i)
            place_core, place_x = i // NX, lax.rem(i, NX)

            @pl.when(i == 0)
            def _():
                loads[2].wait()

            for half in range(2):
                rows = pl.ds(pl.multiple_of((half * 2 * NX + place_x * 2 + place_core) * block, block), block)
                put = pl.ds(pl.multiple_of((i * 2 + half) * block, block), block)
                inputs = pre_act[rows, :].astype(f32)
                cdf = 0.5 * (1.0 + lax.erf(inputs * INV_ROOT_TWO))
                slope[put, :] = cdf + inputs * jnp.exp(-0.5 * inputs * inputs) * INV_ROOT_TAU
                hid_t[:, put] = (inputs * cdf).T.astype(bf16)

        @pl.when(jnp.logical_and(i >= chunks, jnp.logical_and(i < units, lax.rem(i - chunks, 2) == 0)))
        def _():
            c = (i - chunks) // 2
            wait(gbuf.at[c, pl.ds(0, NX * 2 * block)], c_sem.at[c])
            value = jnp.dot(hid_t[...], gbuf[c], preferred_element_type=f32) * scale
            grad[...] = value
            mine[i] = value.astype(bf16)
            send_raw(i)

        @pl.when(jnp.logical_and(lax.rem(i, 2) == 0, jnp.logical_and(i >= B_AT, i < 2 * chunks + B_AT)))
        def _():
            c = (i - B_AT) // 2
            wait(gbuf.at[c, pl.ds(own_at, block)], z_sem.at[c])
            send_x(c, other_at)

            @pl.when(c < chunks - AHEAD)
            def _():
                send_own(c + AHEAD)

        @pl.when(jnp.logical_and(i >= chunks, jnp.logical_and(i < units, lax.rem(i - chunks, 2) == 1)))
        def _():
            c = (i - chunks) // 2

            @pl.when(c == 0)
            def _():
                loads[3].wait()

            value = grad[...]
            mine[i] = (0.95 * second[:, columns(c)] + 0.05 * value * value).astype(bf16)
            send_raw(i)

        @pl.when(jnp.logical_and(lax.rem(i, 2) == 1, jnp.logical_and(i >= C_AT, i < 2 * chunks + C_AT)))
        def _():
            c = (i - C_AT) // 2
            wait(gbuf.at[c, pl.ds(0, 6 * block)], x_sem.at[c])
            part = gbuf.at[c, pl.ds(half_at, NX * 2 * block)]
            send(part, part, cot_send.at[2], c_sem.at[c], c_id)

        u = i - LAG_END

        @pl.when(jnp.logical_and(jnp.logical_not(is_mid), jnp.logical_and(u >= 0, u < units)))
        def _():
            wait(raw.at[u], raw_sem.at[u])
            for r in range(quarter // 16):
                sums = column_slots(u, r)
                for s in range(nslots):
                    slots[u, s, pl.ds(r * 16, 16), :] = sums[s].astype(bf16)
            send(slots.at[u], from_end.at[u], group_send.at[1], end_sem.at[u], mate_id)

        m = i - LAG_MID

        @pl.when(jnp.logical_and(is_mid, jnp.logical_and(m >= 0, m < units)))
        def _():
            wait(raw.at[m], raw_sem.at[m])
            wait(from_end.at[m], end_sem.at[m])
            for r in range(quarter // 16):
                sums = column_slots(m, r)
                for s in range(nslots):
                    rows = pl.ds(r * 16, 16)
                    slots[m, s, rows, :] = (sums[s] + from_end[m, s, rows, :].astype(f32)).astype(bf16)
            send(slots.at[m], from_mid.at[m], group_send.at[1], mid_sem.at[m], mid_id)

        v = i - LAG_AVG

        @pl.when(jnp.logical_and(is_mid, jnp.logical_and(v >= 0, v < units)))
        def _():
            wait(from_mid.at[v], mid_sem.at[v])
            for r in range(quarter // 16):
                rows = pl.ds(r * 16, 16)
                for s in range(nslots):
                    total = slots[v, s, rows, :].astype(f32) + from_mid[v, s, rows, :].astype(f32)
                    avg[v, s, rows, :] = (table[64 + s] * total).astype(bf16)
            send(avg.at[v], from_end.at[v], group_send.at[3], end_sem.at[v], mate_id)
            send_back(v, avg)

        b = i - LAG_RET

        @pl.when(jnp.logical_and(jnp.logical_not(is_mid), jnp.logical_and(b >= 0, b < units)))
        def _():
            wait(from_end.at[b], end_sem.at[b])
            send_back(b, from_end)

        p = i - (units - 1)

        @pl.when(jnp.logical_and(p >= 0, p < 2 * NX))
        def _():
            @pl.when(p == 0)
            def _():
                loads[4].wait()

            here = pl.ds(pl.multiple_of(p * 2 * block, 2 * block), 2 * block)
            total = jnp.zeros((2 * block, pre_act.shape[1]), f32)
            for c in range(chunks):
                total += lax.dot_general(
                    gbuf[c, here, :], w_down[:, c * COLS:(c + 1) * COLS],
                    (((1,), (1,)), ((), ())), preferred_element_type=f32,
                )
            total = (total * slope[here, :]).astype(bf16)
            place_core, place_x = p // NX, lax.rem(p, NX)
            for half in range(2):
                rows = pl.ds(pl.multiple_of((half * 2 * NX + place_x * 2 + place_core) * block, block), block)
                pre[rows, :] = total[half * block:(half + 1) * block]
                pltpu.make_async_copy(pre.at[rows], pre_out.at[rows], store_sem.at[1]).start()

        return carry

    for c in range(AHEAD):
        send_own(c)
    loads[1].wait()
    lax.fori_loop(0, units + LAG_RET, tick, 0)

    wait(gbuf.at[:, pl.ds(0, block)], cot_send.at[0])
    wait(gbuf.at[:, pl.ds(0, 6 * block)], cot_send.at[1])
    wait(gbuf.at[:, pl.ds(0, 2 * NX * block)], cot_send.at[2])
    wait(raw, group_send.at[0])
    wait(slots, group_send.at[1])
    wait(raw, group_send.at[2])
    wait(raw, ret_sem.at[0])
    wait(raw.at[:, 0], store_sem.at[0])
    wait(pre, store_sem.at[1])

    @pl.when(is_mid)
    def _():
        wait(avg, group_send.at[3])


def fill_table(nslots, table, path, counts):
    one, zero = jnp.float32(1.0), jnp.float32(0.0)
    groups = range(NY * NZ)
    paths = [path[g] for g in groups]
    same = {}
    for g in groups:
        for h in range(g):
            same[g, h] = same[h, g] = jnp.where(paths[g] == paths[h], 1, 0)
    opened = jnp.int32(0)
    inverses = [zero] * nslots
    opens, ids = [], []
    for g in groups:
        count = counts[paths[g]]
        inverse = one
        for n in range(2, 9):
            inverse = jnp.where(count == n, jnp.float32(1.0 / n), inverse)
        earlier, spans = jnp.int32(0), jnp.int32(0)
        for h in groups:
            if h < g:
                earlier = jnp.maximum(earlier, same[g, h])
            if h % NZ != g % NZ:
                spans = jnp.maximum(spans, same[g, h])
        open_here = spans * (1 - earlier)
        slot = open_here * opened
        for h in range(g):
            slot += opens[h] * same[g, h] * ids[h]
        opens.append(open_here)
        ids.append(opened)
        for s in range(nslots):
            table[s * 16 + g] = jnp.where(spans * jnp.where(slot == s, 1, 0) == 1, one, zero)
            inverses[s] = jnp.where(open_here * jnp.where(opened == s, 1, 0) == 1, inverse, inverses[s])
        for k in range(NY):
            h = k * NZ + g % NZ
            local = (1 - spans) * (1 if h == g else same[g, h])
            table[80 + g * NY + k] = jnp.where(local == 1, inverse, zero)
        opened = opened + open_here
    for s in range(nslots):
        table[64 + s] = inverses[s]


def slots_needed(path_table):
    ids = jnp.arange(path_table.shape[0], dtype=jnp.int32)
    same = path_table[:, None] == path_table[None, :]
    spans = jnp.any(same & (ids[:, None] % NZ != ids[None, :] % NZ), axis=1)
    earlier = jnp.any(same & (ids[None, :] < ids[:, None]), axis=1)
    return jnp.sum((spans & ~earlier).astype(jnp.int32))


def finish(chunks, means, pre_in, grad_out, first_out, second_out, pre_out):
    f32 = jnp.float32
    for c in range(chunks):
        cols = slice(c * COLS, (c + 1) * COLS)
        grad_mean = means[chunks + 2 * c]
        grad_out[:, cols] = grad_mean
        first_out[:, cols] = 0.9 * means[c].astype(f32) + 0.1 * grad_mean.astype(f32)
        second_out[:, cols] = means[chunks + 2 * c + 1].astype(f32)
    pre_out[...] = pre_in[...]


def exchange(nslots, path_table, sharer_counts, pre_act, cotangent, w_down, first_moment, second_moment):
    f32, bf16 = jnp.float32, jnp.bfloat16
    block, width = cotangent.shape
    tokens, hidden = pre_act.shape
    chunks, quarter = width // COLS, hidden // NY
    units = 3 * chunks
    vmem, hbm = pltpu.VMEM, pl.BlockSpec(memory_space=pl.ANY)
    smem = pl.BlockSpec(memory_space=pltpu.SMEM)
    held = vmem((units, nslots, quarter, COLS), bf16)
    return pl.pallas_call(
        functools.partial(kernel, nslots, chunks, block, quarter, 1.0 / math.sqrt(tokens)),
        out_shape=(
            jax.ShapeDtypeStruct((units, hidden, COLS), bf16),
            jax.ShapeDtypeStruct((tokens, hidden), bf16),
        ),
        in_specs=[smem] * 2 + [hbm] * 5,
        out_specs=(hbm,) * 2,
        scratch_shapes=[
            pltpu.SMEM((144,), f32),
            vmem((tokens, hidden), bf16),
            vmem((block, width), bf16),
            vmem((hidden, width), bf16),
            vmem((hidden, width), f32),
            vmem((hidden, width), f32),
            vmem((chunks, tokens, COLS), bf16),
            vmem((hidden, tokens), bf16),
            vmem((tokens, hidden), f32),
            vmem((hidden, COLS), f32),
            vmem((units, hidden, COLS), bf16),
            vmem((units, 3, quarter, COLS), bf16),
            held,
            held,
            held,
            held,
            vmem((units, 4, quarter, COLS), bf16),
            vmem((tokens, hidden), bf16),
            pltpu.SemaphoreType.DMA((5,)),
            pltpu.SemaphoreType.DMA((2,)),
            pltpu.SemaphoreType.DMA((3,)),
            pltpu.SemaphoreType.DMA((4,)),
            pltpu.SemaphoreType.DMA((chunks,)),
            pltpu.SemaphoreType.DMA((chunks,)),
            pltpu.SemaphoreType.DMA((chunks,)),
            pltpu.SemaphoreType.DMA((units,)),
            pltpu.SemaphoreType.DMA((units,)),
            pltpu.SemaphoreType.DMA((units,)),
            pltpu.SemaphoreType.DMA((1,)),
        ],
        compiler_params=pltpu.CompilerParams(
            collective_id=nslots - FEWEST_SLOTS, has_side_effects=True, vmem_limit_bytes=60 * 2**20
        ),
        cost_estimate=pl.CostEstimate(
            flops=4 * tokens * hidden * width, bytes_accessed=13 * 2**20, transcendentals=2 * tokens * hidden
        ),
        name=f"routed_down_grad_{nslots}",
    )(path_table, sharer_counts, pre_act, cotangent, w_down, first_moment, second_moment)


def per_device(pre_act, cotangent, w_down, first_moment, second_moment, path_table, sharer_counts):
    f32, bf16 = jnp.float32, jnp.bfloat16
    tokens, hidden = pre_act.shape[1:]
    width = cotangent.shape[2]
    chunks = width // COLS
    units = 3 * chunks
    branches = [functools.partial(exchange, n) for n in range(FEWEST_SLOTS, MOST_SLOTS + 1)]
    index = jnp.clip(slots_needed(path_table) - FEWEST_SLOTS, 0, MOST_SLOTS - FEWEST_SLOTS)
    means, pre = lax.switch(
        index, branches, path_table, sharer_counts,
        pre_act[0], cotangent[0], w_down[0], first_moment[0], second_moment[0],
    )
    wide = pl.BlockSpec((hidden // STEPS, width), lambda c: (c, 0))
    tall = pl.BlockSpec((tokens // STEPS, hidden), lambda c: (c, 0))
    outs = pl.pallas_call(
        functools.partial(finish, chunks),
        grid=(STEPS,),
        out_shape=(
            jax.ShapeDtypeStruct((hidden, width), bf16),
            jax.ShapeDtypeStruct((hidden, width), f32),
            jax.ShapeDtypeStruct((hidden, width), f32),
            jax.ShapeDtypeStruct((tokens, hidden), bf16),
        ),
        in_specs=[pl.BlockSpec((units, hidden // STEPS, COLS), lambda c: (0, c, 0)), tall],
        out_specs=(wide, wide, wide, tall),
        compiler_params=pltpu.CompilerParams(vmem_limit_bytes=60 * 2**20),
        name="widen",
    )(means, pre)
    return tuple(out[None] for out in outs)


def solution(mesh):
    placed = (
        P("grp", None, "tp"),
        P("grp", "tp", None),
        P("grp", "tp", None),
        P("grp", "tp", None),
        P("grp", "tp", None),
        P(),
        P(),
    )
    return jax.shard_map(
        per_device,
        mesh=mesh,
        in_specs=placed,
        out_specs=(
            P("grp", "tp", None),
            P("grp", "tp", None),
            P("grp", "tp", None),
            P("grp", None, "tp"),
        ),
        check_vma=False,
    )
```

```python
import functools
import math

import jax
import jax.numpy as jnp
from jax import lax
from jax.experimental import pallas as pl
from jax.experimental.pallas import tpu as pltpu
from jax.sharding import PartitionSpec as P

MESH = pl.DeviceIdType.MESH
COLS = 128
NY = 4
NZ = 4
NX = 4
FEWEST_SLOTS, MOST_SLOTS = 2, 4
LAG_END, LAG_MID, LAG_AVG, LAG_RET = 7, 11, 15, 19

B_AT, C_AT = 10, 15
AHEAD = 4
STEPS = 2

INV_ROOT_TWO = 1.0 / math.sqrt(2.0)
INV_ROOT_TAU = 1.0 / math.sqrt(2.0 * math.pi)


def kernel(
    nslots, chunks, block, quarter, scale,
    path, counts, pre_act_in, cot_in, w_down_in, first_in, second_in,
    ret, pre_out,
    table, pre_act, cot, w_down, first, second,
    gbuf, hid_t, slope, grad, mine, raw, slots, from_end, from_mid, avg, back, pre,
    load_sem, store_sem, cot_send, group_send, z_sem, x_sem, c_sem, raw_sem, end_sem, mid_sem, ret_sem,
):
    f32, bf16 = jnp.float32, jnp.bfloat16
    units = 3 * chunks
    g, t = lax.axis_index("grp"), lax.axis_index("tp")
    y, zl = g // NZ, lax.rem(g, NZ)
    zh, x, core = t // (2 * NX), lax.rem(t // 2, NX), lax.rem(t, 2)
    is_mid = jnp.logical_or(zl == 1, zl == 2)
    mate = jnp.where(is_mid, jnp.where(zl == 1, 0, 3), jnp.where(zl == 0, 1, 2))
    mate_id = (y * NZ + mate, t)
    mid_id = (y * NZ + 3 - zl, t)
    y_ids = [(lax.rem(y + d, NY) * NZ + zl, t) for d in (1, 2, 3)]
    x_ids = [(g, zh * 2 * NX + lax.rem(x + d, NX) * 2 + core) for d in (1, 3, 2)]
    z_id = (g, (1 - zh) * 2 * NX + x * 2 + core)
    c_id = (g, zh * 2 * NX + x * 2 + 1 - core)

    pair_at = pl.multiple_of((core * NX + x) * 2 * block, 2 * block)
    own_at = pl.multiple_of(pair_at + zh * block, block)
    other_at = pl.multiple_of(pair_at + (1 - zh) * block, block)
    half_at = pl.multiple_of(core * NX * 2 * block, NX * 2 * block)

    barrier = pltpu.get_barrier_semaphore()
    for peer in [z_id, c_id, mate_id] + x_ids + y_ids:
        pl.semaphore_signal(barrier, inc=1, device_id=peer, device_id_type=MESH)

    @pl.when(is_mid)
    def _():
        pl.semaphore_signal(barrier, inc=1, device_id=mid_id, device_id_type=MESH)

    loads = [(cot_in, cot), (first_in, first), (pre_act_in, pre_act), (second_in, second), (w_down_in, w_down)]
    loads = [pltpu.make_async_copy(src, dst, load_sem.at[k]) for k, (src, dst) in enumerate(loads)]
    for load in loads:
        load.start()
    fill_table(nslots, table, path, counts)
    loads[0].wait()
    for c in range(chunks):
        gbuf[c, pl.ds(own_at, block), :] = cot[:, c * COLS:(c + 1) * COLS]

    pl.semaphore_wait(barrier, jnp.where(is_mid, 10, 9))

    def send(src, dst, ssem, rsem, peer):
        pltpu.make_async_remote_copy(
            src_ref=src, dst_ref=dst, send_sem=ssem, recv_sem=rsem,
            device_id=peer, device_id_type=MESH,
        ).start()

    def wait(ref, sem):
        pltpu.make_async_copy(ref, ref, sem).wait()

    def columns(c):
        return pl.ds(pl.multiple_of(c * COLS, COLS), COLS)

    def quarter_rows(owner):
        return pl.ds(pl.multiple_of(owner * quarter, quarter), quarter)

    def send_x(c, at):
        part = gbuf.at[c, pl.ds(at, block)]
        for k in range(3):
            send(part, part, cot_send.at[1], x_sem.at[c], x_ids[k])

    def send_own(c):
        part = gbuf.at[c, pl.ds(own_at, block)]
        send(part, part, cot_send.at[0], z_sem.at[c], z_id)
        send_x(c, own_at)

    def send_raw(u):
        for d in range(3):
            owner = lax.rem(y + d + 1, NY)
            send(mine.at[u, quarter_rows(owner)], raw.at[u, d], group_send.at[0], raw_sem.at[u], y_ids[d])

    def column_parts(u, r):
        parts = [mine[u, pl.ds(pl.multiple_of(y * quarter + r * 16, 16), 16), :].astype(f32)]
        return parts + [raw[u, d, pl.ds(r * 16, 16), :].astype(f32) for d in range(3)]

    def column_slots(u, r):
        parts = column_parts(u, r)
        group = [lax.rem(y - d + NY, NY) * NZ + zl for d in range(4)]
        out = []
        for s in range(nslots):
            total = table[s * 16 + group[0]] * parts[0]
            for d in range(1, 4):
                total += table[s * 16 + group[d]] * parts[d]
            out.append(total)
        return out

    def send_back(u, held):
        for r in range(quarter // 16):
            rows = pl.ds(r * 16, 16)
            own = column_parts(u, r)
            parts = [held[u, s, rows, :].astype(f32) for s in range(nslots)]
            for d in range(4):
                group = lax.rem(y + d, NY) * NZ + zl
                total = table[group] * parts[0]
                for s in range(1, nslots):
                    total += table[s * 16 + group] * parts[s]
                for k in range(4):
                    total += table[80 + group * NY + lax.rem(y - k + NY, NY)] * own[k]
                back[u, d, rows, :] = total.astype(bf16)
        pltpu.make_async_copy(back.at[u, 0], ret.at[u, quarter_rows(y)], store_sem.at[0]).start()
        for d in range(3):
            send(back.at[u, d + 1], ret.at[u, quarter_rows(y)], group_send.at[2], ret_sem.at[0], y_ids[d])

    def tick(i, carry):
        @pl.when(i < chunks)
        def _():
            mine[i] = first[:, columns(i)].astype(bf16)
            send_raw(i)

            @pl.when(i == 0)
            def _():
                loads[2].wait()

            for k in range(4 * NX // chunks):
                place = i * (4 * NX // chunks) + k
                owner = lax.rem(place, 2) * 2 * NX + lax.rem(place // 2, NX) * 2 + place // (2 * NX)
                rows = pl.ds(pl.multiple_of(owner * block, block), block)
                put = pl.ds(pl.multiple_of(place * block, block), block)
                inputs = pre_act[rows, :].astype(f32)
                cdf = 0.5 * (1.0 + lax.erf(inputs * INV_ROOT_TWO))
                slope[put, :] = cdf + inputs * jnp.exp(-0.5 * inputs * inputs) * INV_ROOT_TAU
                hid_t[:, put] = (inputs * cdf).T.astype(bf16)

        @pl.when(jnp.logical_and(i >= chunks, jnp.logical_and(i < units, lax.rem(i - chunks, 2) == 0)))
        def _():
            c = (i - chunks) // 2
            wait(gbuf.at[c, pl.ds(0, NX * 2 * block)], c_sem.at[c])
            value = jnp.dot(hid_t[...], gbuf[c], preferred_element_type=f32) * scale
            grad[...] = value
            mine[i] = value.astype(bf16)
            send_raw(i)

        @pl.when(jnp.logical_and(lax.rem(i, 2) == 0, jnp.logical_and(i >= B_AT, i < 2 * chunks + B_AT)))
        def _():
            c = (i - B_AT) // 2
            wait(gbuf.at[c, pl.ds(own_at, block)], z_sem.at[c])
            send_x(c, other_at)

            @pl.when(c < chunks - AHEAD)
            def _():
                send_own(c + AHEAD)

        @pl.when(jnp.logical_and(i >= chunks, jnp.logical_and(i < units, lax.rem(i - chunks, 2) == 1)))
        def _():
            c = (i - chunks) // 2

            @pl.when(c == 0)
            def _():
                loads[3].wait()

            value = grad[...]
            mine[i] = (0.95 * second[:, columns(c)] + 0.05 * value * value).astype(bf16)
            send_raw(i)

        @pl.when(jnp.logical_and(lax.rem(i, 2) == 1, jnp.logical_and(i >= C_AT, i < 2 * chunks + C_AT)))
        def _():
            c = (i - C_AT) // 2
            wait(gbuf.at[c, pl.ds(0, 6 * block)], x_sem.at[c])
            part = gbuf.at[c, pl.ds(half_at, NX * 2 * block)]
            send(part, part, cot_send.at[2], c_sem.at[c], c_id)

        u = i - LAG_END

        @pl.when(jnp.logical_and(jnp.logical_not(is_mid), jnp.logical_and(u >= 0, u < units)))
        def _():
            wait(raw.at[u], raw_sem.at[u])
            for r in range(quarter // 16):
                sums = column_slots(u, r)
                for s in range(nslots):
                    slots[u, s, pl.ds(r * 16, 16), :] = sums[s].astype(bf16)
            send(slots.at[u], from_end.at[u], group_send.at[1], end_sem.at[u], mate_id)

        m = i - LAG_MID

        @pl.when(jnp.logical_and(is_mid, jnp.logical_and(m >= 0, m < units)))
        def _():
            wait(raw.at[m], raw_sem.at[m])
            wait(from_end.at[m], end_sem.at[m])
            for r in range(quarter // 16):
                sums = column_slots(m, r)
                for s in range(nslots):
                    rows = pl.ds(r * 16, 16)
                    slots[m, s, rows, :] = (sums[s] + from_end[m, s, rows, :].astype(f32)).astype(bf16)
            send(slots.at[m], from_mid.at[m], group_send.at[1], mid_sem.at[m], mid_id)

        v = i - LAG_AVG

        @pl.when(jnp.logical_and(is_mid, jnp.logical_and(v >= 0, v < units)))
        def _():
            wait(from_mid.at[v], mid_sem.at[v])
            for r in range(quarter // 16):
                rows = pl.ds(r * 16, 16)
                for s in range(nslots):
                    total = slots[v, s, rows, :].astype(f32) + from_mid[v, s, rows, :].astype(f32)
                    avg[v, s, rows, :] = (table[64 + s] * total).astype(bf16)
            send(avg.at[v], from_end.at[v], group_send.at[3], end_sem.at[v], mate_id)
            send_back(v, avg)

        b = i - LAG_RET

        @pl.when(jnp.logical_and(jnp.logical_not(is_mid), jnp.logical_and(b >= 0, b < units)))
        def _():
            wait(from_end.at[b], end_sem.at[b])
            send_back(b, from_end)

        p = i - (units - 1)

        @pl.when(jnp.logical_and(p >= 0, p < 2 * NX))
        def _():
            @pl.when(p == 0)
            def _():
                loads[4].wait()

            here = pl.ds(pl.multiple_of(p * 2 * block, 2 * block), 2 * block)
            total = jnp.zeros((2 * block, pre_act.shape[1]), f32)
            for c in range(chunks):
                total += lax.dot_general(
                    gbuf[c, here, :], w_down[:, c * COLS:(c + 1) * COLS],
                    (((1,), (1,)), ((), ())), preferred_element_type=f32,
                )
            total = (total * slope[here, :]).astype(bf16)
            place_core, place_x = p // NX, lax.rem(p, NX)
            for half in range(2):
                rows = pl.ds(pl.multiple_of((half * 2 * NX + place_x * 2 + place_core) * block, block), block)
                pre[rows, :] = total[half * block:(half + 1) * block]
                pltpu.make_async_copy(pre.at[rows], pre_out.at[rows], store_sem.at[1]).start()

        return carry

    for c in range(AHEAD):
        send_own(c)
    loads[1].wait()
    lax.fori_loop(0, units + max(LAG_RET, 2 * NX - 1), tick, 0)

    wait(gbuf.at[:, pl.ds(0, block)], cot_send.at[0])
    wait(gbuf.at[:, pl.ds(0, 6 * block)], cot_send.at[1])
    wait(gbuf.at[:, pl.ds(0, 2 * NX * block)], cot_send.at[2])
    wait(raw, group_send.at[0])
    wait(slots, group_send.at[1])
    wait(raw, group_send.at[2])
    wait(raw, ret_sem.at[0])
    wait(raw.at[:, 0], store_sem.at[0])
    wait(pre, store_sem.at[1])

    @pl.when(is_mid)
    def _():
        wait(avg, group_send.at[3])


def fill_table(nslots, table, path, counts):
    one, zero = jnp.float32(1.0), jnp.float32(0.0)
    groups = range(NY * NZ)
    paths = [path[g] for g in groups]
    same = {}
    for g in groups:
        for h in range(g):
            same[g, h] = same[h, g] = jnp.where(paths[g] == paths[h], 1, 0)
    opened = jnp.int32(0)
    inverses = [zero] * nslots
    opens, ids = [], []
    for g in groups:
        count = counts[paths[g]]
        inverse = one
        for n in range(2, 9):
            inverse = jnp.where(count == n, jnp.float32(1.0 / n), inverse)
        earlier, spans = jnp.int32(0), jnp.int32(0)
        for h in groups:
            if h < g:
                earlier = jnp.maximum(earlier, same[g, h])
            if h % NZ != g % NZ:
                spans = jnp.maximum(spans, same[g, h])
        open_here = spans * (1 - earlier)
        slot = open_here * opened
        for h in range(g):
            slot += opens[h] * same[g, h] * ids[h]
        opens.append(open_here)
        ids.append(opened)
        for s in range(nslots):
            table[s * 16 + g] = jnp.where(spans * jnp.where(slot == s, 1, 0) == 1, one, zero)
            inverses[s] = jnp.where(open_here * jnp.where(opened == s, 1, 0) == 1, inverse, inverses[s])
        for k in range(NY):
            h = k * NZ + g % NZ
            local = (1 - spans) * (1 if h == g else same[g, h])
            table[80 + g * NY + k] = jnp.where(local == 1, inverse, zero)
        opened = opened + open_here
    for s in range(nslots):
        table[64 + s] = inverses[s]


def slots_needed(path_table):
    ids = jnp.arange(path_table.shape[0], dtype=jnp.int32)
    same = path_table[:, None] == path_table[None, :]
    spans = jnp.any(same & (ids[:, None] % NZ != ids[None, :] % NZ), axis=1)
    earlier = jnp.any(same & (ids[None, :] < ids[:, None]), axis=1)
    return jnp.sum((spans & ~earlier).astype(jnp.int32))


def finish(chunks, means, pre_in, grad_out, first_out, second_out, pre_out):
    f32 = jnp.float32
    for c in range(chunks):
        cols = slice(c * COLS, (c + 1) * COLS)
        grad_mean = means[chunks + 2 * c]
        grad_out[:, cols] = grad_mean
        first_out[:, cols] = 0.9 * means[c].astype(f32) + 0.1 * grad_mean.astype(f32)
        second_out[:, cols] = means[chunks + 2 * c + 1].astype(f32)
    pre_out[...] = pre_in[...]


def exchange(nslots, path_table, sharer_counts, pre_act, cotangent, w_down, first_moment, second_moment):
    f32, bf16 = jnp.float32, jnp.bfloat16
    block, width = cotangent.shape
    tokens, hidden = pre_act.shape
    chunks, quarter = width // COLS, hidden // NY
    units = 3 * chunks
    vmem, hbm = pltpu.VMEM, pl.BlockSpec(memory_space=pl.ANY)
    smem = pl.BlockSpec(memory_space=pltpu.SMEM)
    held = vmem((units, nslots, quarter, COLS), bf16)
    return pl.pallas_call(
        functools.partial(kernel, nslots, chunks, block, quarter, 1.0 / math.sqrt(tokens)),
        out_shape=(
            jax.ShapeDtypeStruct((units, hidden, COLS), bf16),
            jax.ShapeDtypeStruct((tokens, hidden), bf16),
        ),
        in_specs=[smem] * 2 + [hbm] * 5,
        out_specs=(hbm,) * 2,
        scratch_shapes=[
            pltpu.SMEM((144,), f32),
            vmem((tokens, hidden), bf16),
            vmem((block, width), bf16),
            vmem((hidden, width), bf16),
            vmem((hidden, width), f32),
            vmem((hidden, width), f32),
            vmem((chunks, tokens, COLS), bf16),
            vmem((hidden, tokens), bf16),
            vmem((tokens, hidden), f32),
            vmem((hidden, COLS), f32),
            vmem((units, hidden, COLS), bf16),
            vmem((units, 3, quarter, COLS), bf16),
            held,
            held,
            held,
            held,
            vmem((units, 4, quarter, COLS), bf16),
            vmem((tokens, hidden), bf16),
            pltpu.SemaphoreType.DMA((5,)),
            pltpu.SemaphoreType.DMA((2,)),
            pltpu.SemaphoreType.DMA((3,)),
            pltpu.SemaphoreType.DMA((4,)),
            pltpu.SemaphoreType.DMA((chunks,)),
            pltpu.SemaphoreType.DMA((chunks,)),
            pltpu.SemaphoreType.DMA((chunks,)),
            pltpu.SemaphoreType.DMA((units,)),
            pltpu.SemaphoreType.DMA((units,)),
            pltpu.SemaphoreType.DMA((units,)),
            pltpu.SemaphoreType.DMA((1,)),
        ],
        compiler_params=pltpu.CompilerParams(
            collective_id=nslots - FEWEST_SLOTS, has_side_effects=True, vmem_limit_bytes=60 * 2**20
        ),
        cost_estimate=pl.CostEstimate(
            flops=4 * tokens * hidden * width, bytes_accessed=13 * 2**20, transcendentals=2 * tokens * hidden
        ),
        name=f"routed_down_grad_{nslots}",
    )(path_table, sharer_counts, pre_act, cotangent, w_down, first_moment, second_moment)


def per_device(pre_act, cotangent, w_down, first_moment, second_moment, path_table, sharer_counts):
    f32, bf16 = jnp.float32, jnp.bfloat16
    tokens, hidden = pre_act.shape[1:]
    width = cotangent.shape[2]
    chunks = width // COLS
    units = 3 * chunks
    branches = [functools.partial(exchange, n) for n in range(FEWEST_SLOTS, MOST_SLOTS + 1)]
    index = jnp.clip(slots_needed(path_table) - FEWEST_SLOTS, 0, MOST_SLOTS - FEWEST_SLOTS)
    means, pre = lax.switch(
        index, branches, path_table, sharer_counts,
        pre_act[0], cotangent[0], w_down[0], first_moment[0], second_moment[0],
    )
    wide = pl.BlockSpec((hidden // STEPS, width), lambda c: (c, 0))
    tall = pl.BlockSpec((tokens // STEPS, hidden), lambda c: (c, 0))
    outs = pl.pallas_call(
        functools.partial(finish, chunks),
        grid=(STEPS,),
        out_shape=(
            jax.ShapeDtypeStruct((hidden, width), bf16),
            jax.ShapeDtypeStruct((hidden, width), f32),
            jax.ShapeDtypeStruct((hidden, width), f32),
            jax.ShapeDtypeStruct((tokens, hidden), bf16),
        ),
        in_specs=[pl.BlockSpec((units, hidden // STEPS, COLS), lambda c: (0, c, 0)), tall],
        out_specs=(wide, wide, wide, tall),
        compiler_params=pltpu.CompilerParams(vmem_limit_bytes=60 * 2**20),
        name="widen",
    )(means, pre)
    return tuple(out[None] for out in outs)


def solution(mesh):
    placed = (
        P("grp", None, "tp"),
        P("grp", "tp", None),
        P("grp", "tp", None),
        P("grp", "tp", None),
        P("grp", "tp", None),
        P(),
        P(),
    )
    return jax.shard_map(
        per_device,
        mesh=mesh,
        in_specs=placed,
        out_specs=(
            P("grp", "tp", None),
            P("grp", "tp", None),
            P("grp", "tp", None),
            P("grp", None, "tp"),
        ),
        check_vma=False,
    )
```

```python
import functools
import math

import jax
import jax.numpy as jnp
from jax import lax
from jax.experimental import pallas as pl
from jax.experimental.pallas import tpu as pltpu
from jax.sharding import PartitionSpec as P

MESH = pl.DeviceIdType.MESH
COLS = 128
NY = 4
NZ = 4
NX = 4
FEWEST_SLOTS, MOST_SLOTS = 2, 4
LAG_END, LAG_MID, LAG_AVG, LAG_RET = 7, 11, 15, 19

B_AT, C_AT = 10, 15
AHEAD = 4
STEPS = 4

INV_ROOT_TWO = 1.0 / math.sqrt(2.0)
INV_ROOT_TAU = 1.0 / math.sqrt(2.0 * math.pi)


def kernel(
    nslots, chunks, block, quarter, scale,
    path, counts, pre_act_in, cot_in, w_down_in, first_in, second_in,
    ret, pre_out,
    table, pre_act, cot, w_down, first, second,
    gbuf, hid_t, slope, grad, mine, raw, slots, from_end, from_mid, avg, back, pre,
    load_sem, store_sem, cot_send, group_send, z_sem, x_sem, c_sem, raw_sem, end_sem, mid_sem, ret_sem,
):
    f32, bf16 = jnp.float32, jnp.bfloat16
    units = 3 * chunks
    g, t = lax.axis_index("grp"), lax.axis_index("tp")
    y, zl = g // NZ, lax.rem(g, NZ)
    zh, x, core = t // (2 * NX), lax.rem(t // 2, NX), lax.rem(t, 2)
    is_mid = jnp.logical_or(zl == 1, zl == 2)
    mate = jnp.where(is_mid, jnp.where(zl == 1, 0, 3), jnp.where(zl == 0, 1, 2))
    mate_id = (y * NZ + mate, t)
    mid_id = (y * NZ + 3 - zl, t)
    y_ids = [(lax.rem(y + d, NY) * NZ + zl, t) for d in (1, 2, 3)]
    x_ids = [(g, zh * 2 * NX + lax.rem(x + d, NX) * 2 + core) for d in (1, 3, 2)]
    z_id = (g, (1 - zh) * 2 * NX + x * 2 + core)
    c_id = (g, zh * 2 * NX + x * 2 + 1 - core)

    pair_at = pl.multiple_of((core * NX + x) * 2 * block, 2 * block)
    own_at = pl.multiple_of(pair_at + zh * block, block)
    other_at = pl.multiple_of(pair_at + (1 - zh) * block, block)
    half_at = pl.multiple_of(core * NX * 2 * block, NX * 2 * block)

    barrier = pltpu.get_barrier_semaphore()
    for peer in [z_id, c_id, mate_id] + x_ids + y_ids:
        pl.semaphore_signal(barrier, inc=1, device_id=peer, device_id_type=MESH)

    @pl.when(is_mid)
    def _():
        pl.semaphore_signal(barrier, inc=1, device_id=mid_id, device_id_type=MESH)

    loads = [(cot_in, cot), (first_in, first), (pre_act_in, pre_act), (second_in, second), (w_down_in, w_down)]
    loads = [pltpu.make_async_copy(src, dst, load_sem.at[k]) for k, (src, dst) in enumerate(loads)]
    for load in loads:
        load.start()
    fill_table(nslots, table, path, counts)
    loads[0].wait()
    for c in range(chunks):
        gbuf[c, pl.ds(own_at, block), :] = cot[:, c * COLS:(c + 1) * COLS]

    pl.semaphore_wait(barrier, jnp.where(is_mid, 10, 9))

    def send(src, dst, ssem, rsem, peer):
        pltpu.make_async_remote_copy(
            src_ref=src, dst_ref=dst, send_sem=ssem, recv_sem=rsem,
            device_id=peer, device_id_type=MESH,
        ).start()

    def wait(ref, sem):
        pltpu.make_async_copy(ref, ref, sem).wait()

    def columns(c):
        return pl.ds(pl.multiple_of(c * COLS, COLS), COLS)

    def quarter_rows(owner):
        return pl.ds(pl.multiple_of(owner * quarter, quarter), quarter)

    def send_x(c, at):
        part = gbuf.at[c, pl.ds(at, block)]
        for k in range(3):
            send(part, part, cot_send.at[1], x_sem.at[c], x_ids[k])

    def send_own(c):
        part = gbuf.at[c, pl.ds(own_at, block)]
        send(part, part, cot_send.at[0], z_sem.at[c], z_id)
        send_x(c, own_at)

    def send_raw(u):
        for d in range(3):
            owner = lax.rem(y + d + 1, NY)
            send(mine.at[u, quarter_rows(owner)], raw.at[u, d], group_send.at[0], raw_sem.at[u], y_ids[d])

    def column_parts(u, r):
        parts = [mine[u, pl.ds(pl.multiple_of(y * quarter + r * 16, 16), 16), :].astype(f32)]
        return parts + [raw[u, d, pl.ds(r * 16, 16), :].astype(f32) for d in range(3)]

    def column_slots(u, r):
        parts = column_parts(u, r)
        group = [lax.rem(y - d + NY, NY) * NZ + zl for d in range(4)]
        out = []
        for s in range(nslots):
            total = table[s * 16 + group[0]] * parts[0]
            for d in range(1, 4):
                total += table[s * 16 + group[d]] * parts[d]
            out.append(total)
        return out

    def send_back(u, held):
        for r in range(quarter // 16):
            rows = pl.ds(r * 16, 16)
            own = column_parts(u, r)
            parts = [held[u, s, rows, :].astype(f32) for s in range(nslots)]
            for d in range(4):
                group = lax.rem(y + d, NY) * NZ + zl
                total = table[group] * parts[0]
                for s in range(1, nslots):
                    total += table[s * 16 + group] * parts[s]
                for k in range(4):
                    total += table[80 + group * NY + lax.rem(y - k + NY, NY)] * own[k]
                back[u, d, rows, :] = total.astype(bf16)
        pltpu.make_async_copy(back.at[u, 0], ret.at[u, quarter_rows(y)], store_sem.at[0]).start()
        for d in range(3):
            send(back.at[u, d + 1], ret.at[u, quarter_rows(y)], group_send.at[2], ret_sem.at[0], y_ids[d])

    def tick(i, carry):
        @pl.when(i < chunks)
        def _():
            mine[i] = first[:, columns(i)].astype(bf16)
            send_raw(i)

            @pl.when(i == 0)
            def _():
                loads[2].wait()

            for k in range(4 * NX // chunks):
                place = i * (4 * NX // chunks) + k
                owner = lax.rem(place, 2) * 2 * NX + lax.rem(place // 2, NX) * 2 + place // (2 * NX)
                rows = pl.ds(pl.multiple_of(owner * block, block), block)
                put = pl.ds(pl.multiple_of(place * block, block), block)
                inputs = pre_act[rows, :].astype(f32)
                cdf = 0.5 * (1.0 + lax.erf(inputs * INV_ROOT_TWO))
                slope[put, :] = cdf + inputs * jnp.exp(-0.5 * inputs * inputs) * INV_ROOT_TAU
                hid_t[:, put] = (inputs * cdf).T.astype(bf16)

        @pl.when(jnp.logical_and(i >= chunks, jnp.logical_and(i < units, lax.rem(i - chunks, 2) == 0)))
        def _():
            c = (i - chunks) // 2
            wait(gbuf.at[c, pl.ds(0, NX * 2 * block)], c_sem.at[c])
            value = jnp.dot(hid_t[...], gbuf[c], preferred_element_type=f32) * scale
            grad[...] = value
            mine[i] = value.astype(bf16)
            send_raw(i)

        @pl.when(jnp.logical_and(lax.rem(i, 2) == 0, jnp.logical_and(i >= B_AT, i < 2 * chunks + B_AT)))
        def _():
            c = (i - B_AT) // 2
            wait(gbuf.at[c, pl.ds(own_at, block)], z_sem.at[c])
            send_x(c, other_at)

            @pl.when(c < chunks - AHEAD)
            def _():
                send_own(c + AHEAD)

        @pl.when(jnp.logical_and(i >= chunks, jnp.logical_and(i < units, lax.rem(i - chunks, 2) == 1)))
        def _():
            c = (i - chunks) // 2

            @pl.when(c == 0)
            def _():
                loads[3].wait()

            value = grad[...]
            mine[i] = (0.95 * second[:, columns(c)] + 0.05 * value * value).astype(bf16)
            send_raw(i)

        @pl.when(jnp.logical_and(lax.rem(i, 2) == 1, jnp.logical_and(i >= C_AT, i < 2 * chunks + C_AT)))
        def _():
            c = (i - C_AT) // 2
            wait(gbuf.at[c, pl.ds(0, 6 * block)], x_sem.at[c])
            part = gbuf.at[c, pl.ds(half_at, NX * 2 * block)]
            send(part, part, cot_send.at[2], c_sem.at[c], c_id)

        u = i - LAG_END

        @pl.when(jnp.logical_and(jnp.logical_not(is_mid), jnp.logical_and(u >= 0, u < units)))
        def _():
            wait(raw.at[u], raw_sem.at[u])
            for r in range(quarter // 16):
                sums = column_slots(u, r)
                for s in range(nslots):
                    slots[u, s, pl.ds(r * 16, 16), :] = sums[s].astype(bf16)
            send(slots.at[u], from_end.at[u], group_send.at[1], end_sem.at[u], mate_id)

        m = i - LAG_MID

        @pl.when(jnp.logical_and(is_mid, jnp.logical_and(m >= 0, m < units)))
        def _():
            wait(raw.at[m], raw_sem.at[m])
            wait(from_end.at[m], end_sem.at[m])
            for r in range(quarter // 16):
                sums = column_slots(m, r)
                for s in range(nslots):
                    rows = pl.ds(r * 16, 16)
                    slots[m, s, rows, :] = (sums[s] + from_end[m, s, rows, :].astype(f32)).astype(bf16)
            send(slots.at[m], from_mid.at[m], group_send.at[1], mid_sem.at[m], mid_id)

        v = i - LAG_AVG

        @pl.when(jnp.logical_and(is_mid, jnp.logical_and(v >= 0, v < units)))
        def _():
            wait(from_mid.at[v], mid_sem.at[v])
            for r in range(quarter // 16):
                rows = pl.ds(r * 16, 16)
                for s in range(nslots):
                    total = slots[v, s, rows, :].astype(f32) + from_mid[v, s, rows, :].astype(f32)
                    avg[v, s, rows, :] = (table[64 + s] * total).astype(bf16)
            send(avg.at[v], from_end.at[v], group_send.at[3], end_sem.at[v], mate_id)
            send_back(v, avg)

        b = i - LAG_RET

        @pl.when(jnp.logical_and(jnp.logical_not(is_mid), jnp.logical_and(b >= 0, b < units)))
        def _():
            wait(from_end.at[b], end_sem.at[b])
            send_back(b, from_end)

        p = i - (units + LAG_RET - 2 * NX)

        @pl.when(jnp.logical_and(p >= 0, p < 2 * NX))
        def _():
            @pl.when(p == 0)
            def _():
                loads[4].wait()

            here = pl.ds(pl.multiple_of(p * 2 * block, 2 * block), 2 * block)
            total = jnp.zeros((2 * block, pre_act.shape[1]), f32)
            for c in range(chunks):
                total += lax.dot_general(
                    gbuf[c, here, :], w_down[:, c * COLS:(c + 1) * COLS],
                    (((1,), (1,)), ((), ())), preferred_element_type=f32,
                )
            total = (total * slope[here, :]).astype(bf16)
            place_core, place_x = p // NX, lax.rem(p, NX)
            for half in range(2):
                rows = pl.ds(pl.multiple_of((half * 2 * NX + place_x * 2 + place_core) * block, block), block)
                pre[rows, :] = total[half * block:(half + 1) * block]
                pltpu.make_async_copy(pre.at[rows], pre_out.at[rows], store_sem.at[1]).start()

        return carry

    for c in range(AHEAD):
        send_own(c)
    loads[1].wait()
    lax.fori_loop(0, units + LAG_RET, tick, 0)

    wait(gbuf.at[:, pl.ds(0, block)], cot_send.at[0])
    wait(gbuf.at[:, pl.ds(0, 6 * block)], cot_send.at[1])
    wait(gbuf.at[:, pl.ds(0, 2 * NX * block)], cot_send.at[2])
    wait(raw, group_send.at[0])
    wait(slots, group_send.at[1])
    wait(raw, group_send.at[2])
    wait(raw, ret_sem.at[0])
    wait(raw.at[:, 0], store_sem.at[0])
    wait(pre, store_sem.at[1])

    @pl.when(is_mid)
    def _():
        wait(avg, group_send.at[3])


def fill_table(nslots, table, path, counts):
    one, zero = jnp.float32(1.0), jnp.float32(0.0)
    groups = range(NY * NZ)
    paths = [path[g] for g in groups]
    same = {}
    for g in groups:
        for h in range(g):
            same[g, h] = same[h, g] = jnp.where(paths[g] == paths[h], 1, 0)
    opened = jnp.int32(0)
    inverses = [zero] * nslots
    opens, ids = [], []
    for g in groups:
        count = counts[paths[g]]
        inverse = one
        for n in range(2, 9):
            inverse = jnp.where(count == n, jnp.float32(1.0 / n), inverse)
        earlier, spans = jnp.int32(0), jnp.int32(0)
        for h in groups:
            if h < g:
                earlier = jnp.maximum(earlier, same[g, h])
            if h % NZ != g % NZ:
                spans = jnp.maximum(spans, same[g, h])
        open_here = spans * (1 - earlier)
        slot = open_here * opened
        for h in range(g):
            slot += opens[h] * same[g, h] * ids[h]
        opens.append(open_here)
        ids.append(opened)
        for s in range(nslots):
            table[s * 16 + g] = jnp.where(spans * jnp.where(slot == s, 1, 0) == 1, one, zero)
            inverses[s] = jnp.where(open_here * jnp.where(opened == s, 1, 0) == 1, inverse, inverses[s])
        for k in range(NY):
            h = k * NZ + g % NZ
            local = (1 - spans) * (1 if h == g else same[g, h])
            table[80 + g * NY + k] = jnp.where(local == 1, inverse, zero)
        opened = opened + open_here
    for s in range(nslots):
        table[64 + s] = inverses[s]


def slots_needed(path_table):
    ids = jnp.arange(path_table.shape[0], dtype=jnp.int32)
    same = path_table[:, None] == path_table[None, :]
    spans = jnp.any(same & (ids[:, None] % NZ != ids[None, :] % NZ), axis=1)
    earlier = jnp.any(same & (ids[None, :] < ids[:, None]), axis=1)
    return jnp.sum((spans & ~earlier).astype(jnp.int32))


def finish(chunks, means, pre_in, grad_out, first_out, second_out, pre_out, grad, first, second, pre, sem):
    f32 = jnp.float32
    load = pltpu.make_async_copy(pre_in, pre, sem.at[3])
    store = pltpu.make_async_copy(pre, pre_out, sem.at[4])
    load.start()
    depth = grad.shape[0] // STEPS
    for r in range(STEPS):
        rows = slice(r * depth, (r + 1) * depth)
        for c in range(chunks):
            cols = slice(c * COLS, (c + 1) * COLS)
            grad_mean = means[chunks + 2 * c, rows, :]
            grad[rows, cols] = grad_mean
            first[rows, cols] = 0.9 * means[c, rows, :].astype(f32) + 0.1 * grad_mean.astype(f32)
            second[rows, cols] = means[chunks + 2 * c + 1, rows, :].astype(f32)
        for k, (held, out) in enumerate(((grad, grad_out), (first, first_out), (second, second_out))):
            pltpu.make_async_copy(held.at[rows], out.at[rows], sem.at[k]).start()
    load.wait()
    store.start()
    for k, held in enumerate((grad, first, second)):
        pltpu.make_async_copy(held, held, sem.at[k]).wait()
    store.wait()


def exchange(nslots, path_table, sharer_counts, pre_act, cotangent, w_down, first_moment, second_moment):
    f32, bf16 = jnp.float32, jnp.bfloat16
    block, width = cotangent.shape
    tokens, hidden = pre_act.shape
    chunks, quarter = width // COLS, hidden // NY
    units = 3 * chunks
    vmem, hbm = pltpu.VMEM, pl.BlockSpec(memory_space=pl.ANY)
    smem = pl.BlockSpec(memory_space=pltpu.SMEM)
    held = vmem((units, nslots, quarter, COLS), bf16)
    return pl.pallas_call(
        functools.partial(kernel, nslots, chunks, block, quarter, 1.0 / math.sqrt(tokens)),
        out_shape=(
            jax.ShapeDtypeStruct((units, hidden, COLS), bf16),
            jax.ShapeDtypeStruct((tokens, hidden), bf16),
        ),
        in_specs=[smem] * 2 + [hbm] * 5,
        out_specs=(hbm,) * 2,
        scratch_shapes=[
            pltpu.SMEM((144,), f32),
            vmem((tokens, hidden), bf16),
            vmem((block, width), bf16),
            vmem((hidden, width), bf16),
            vmem((hidden, width), f32),
            vmem((hidden, width), f32),
            vmem((chunks, tokens, COLS), bf16),
            vmem((hidden, tokens), bf16),
            vmem((tokens, hidden), f32),
            vmem((hidden, COLS), f32),
            vmem((units, hidden, COLS), bf16),
            vmem((units, 3, quarter, COLS), bf16),
            held,
            held,
            held,
            held,
            vmem((units, 4, quarter, COLS), bf16),
            vmem((tokens, hidden), bf16),
            pltpu.SemaphoreType.DMA((5,)),
            pltpu.SemaphoreType.DMA((2,)),
            pltpu.SemaphoreType.DMA((3,)),
            pltpu.SemaphoreType.DMA((4,)),
            pltpu.SemaphoreType.DMA((chunks,)),
            pltpu.SemaphoreType.DMA((chunks,)),
            pltpu.SemaphoreType.DMA((chunks,)),
            pltpu.SemaphoreType.DMA((units,)),
            pltpu.SemaphoreType.DMA((units,)),
            pltpu.SemaphoreType.DMA((units,)),
            pltpu.SemaphoreType.DMA((1,)),
        ],
        compiler_params=pltpu.CompilerParams(
            collective_id=nslots - FEWEST_SLOTS, has_side_effects=True, vmem_limit_bytes=60 * 2**20
        ),
        cost_estimate=pl.CostEstimate(
            flops=4 * tokens * hidden * width, bytes_accessed=13 * 2**20, transcendentals=2 * tokens * hidden
        ),
        name=f"routed_down_grad_{nslots}",
    )(path_table, sharer_counts, pre_act, cotangent, w_down, first_moment, second_moment)


def per_device(pre_act, cotangent, w_down, first_moment, second_moment, path_table, sharer_counts):
    f32, bf16 = jnp.float32, jnp.bfloat16
    tokens, hidden = pre_act.shape[1:]
    width = cotangent.shape[2]
    chunks = width // COLS
    branches = [functools.partial(exchange, n) for n in range(FEWEST_SLOTS, MOST_SLOTS + 1)]
    index = jnp.clip(slots_needed(path_table) - FEWEST_SLOTS, 0, MOST_SLOTS - FEWEST_SLOTS)
    means, pre = lax.switch(
        index, branches, path_table, sharer_counts,
        pre_act[0], cotangent[0], w_down[0], first_moment[0], second_moment[0],
    )
    hbm = pl.BlockSpec(memory_space=pl.ANY)
    outs = pl.pallas_call(
        functools.partial(finish, chunks),
        out_shape=(
            jax.ShapeDtypeStruct((hidden, width), bf16),
            jax.ShapeDtypeStruct((hidden, width), f32),
            jax.ShapeDtypeStruct((hidden, width), f32),
            jax.ShapeDtypeStruct((tokens, hidden), bf16),
        ),
        in_specs=[pl.BlockSpec(memory_space=pltpu.VMEM), hbm],
        out_specs=(hbm,) * 4,
        scratch_shapes=[
            pltpu.VMEM((hidden, width), bf16),
            pltpu.VMEM((hidden, width), f32),
            pltpu.VMEM((hidden, width), f32),
            pltpu.VMEM((tokens, hidden), bf16),
            pltpu.SemaphoreType.DMA((5,)),
        ],
        compiler_params=pltpu.CompilerParams(vmem_limit_bytes=60 * 2**20),
        name="widen",
    )(means, pre)
    return tuple(out[None] for out in outs)


def solution(mesh):
    placed = (
        P("grp", None, "tp"),
        P("grp", "tp", None),
        P("grp", "tp", None),
        P("grp", "tp", None),
        P("grp", "tp", None),
        P(),
        P(),
    )
    return jax.shard_map(
        per_device,
        mesh=mesh,
        in_specs=placed,
        out_specs=(
            P("grp", "tp", None),
            P("grp", "tp", None),
            P("grp", "tp", None),
            P("grp", None, "tp"),
        ),
        check_vma=False,
    )
```
